32 devices in a mesh: seq: 4 (over y, x), tp: 8 (over z, core).
Axes of the slice: x: 2, y: 2, z: 4, core: 2. Of those that a mesh axis runs over, the one named last changes fastest.
Arguments:
- query: bfloat16 [4096, 8192], P('seq', 'tp'), may hold values from -6 to 6
- key_in: bfloat16 [4096, 8192], P('seq', 'tp'), may hold values from -6 to 6
- value: bfloat16 [4096, 8192], P('seq', 'tp'), may hold values from -6 to 6
- gate: bfloat16 [4096, 8192], P('seq', 'tp'), may hold values from -8 to 8
- kv_start: float32 [64, 128, 128], P('tp'), may hold values from -240 to 240
- norm_gain: float32 [8192], P('tp'), may hold values from 0.5 to 2
- w_out: bfloat16 [8192, 6144], P('tp'), may hold values from -0.0625 to 0.0625
Outputs:
- mixed: bfloat16 [4096, 6144], P(('seq', 'tp'))
The draws below stay inside these ranges and needn't reach their ends.
All inputs are finite; a program needn't handle non-finite values.
Results may differ from the reference program's by a relative error of at most 0.019.
Values may be sent and summed in bfloat16 or wider, within the bound.
A program may use at most 128 MiB of HBM per device.

```python
import math
import jax
import jax.numpy as jnp
from jax import lax

D = 6144
H = 64
HD = 128
TOK_DEV = 1024
TOKENS = 4096
N_TP = 8


def level_of(key, extent, split, least, high):
    loudness = 1.0
    for axis_at, parts in split:
        draws = jax.random.uniform(jax.random.fold_in(jax.random.fold_in(key, 6), axis_at), (parts,), jnp.float32, least / len(split), high / len(split))
        loudness = loudness * jnp.repeat(jnp.exp(draws), extent[axis_at] // parts).reshape((-1,) + (1,) * (len(extent) - 1 - axis_at))
    return loudness


def noise(own_key, dims, scale, most, pieces=(), held_as=jnp.bfloat16):
    drawn = jax.random.normal(own_key, dims, jnp.float32) * scale
    if len(pieces) > 0:
        drawn = level_of(own_key, dims, pieces, -0.22, 0.18) * drawn
    return jnp.clip(drawn, min=-most, max=most).astype(held_as)


def setup_inputs(seed: int = 0) -> dict:
    splits = jax.random.split(jax.random.key(seed), 8)
    query = noise(splits[0], (TOKENS, H * HD), 1.0, 6.0, ((0, 4), (1, 8)))
    key_in = noise(splits[1], (TOKENS, H * HD), 1.0, 6.0, ((0, 4), (1, 8)))
    value = noise(splits[2], (TOKENS, H * HD), 1.0, 6.0, ((0, 4), (1, 8)))
    gate = noise(splits[3], (TOKENS, H * HD), 1.5, 8.0, ((0, 4), (1, 8)))
    kv_start = noise(splits[4], (H, HD, HD), 40.0, 240.0, ((0, 8),), jnp.float32)
    norm_gain = jnp.clip(jnp.exp(math.log(2.0) - 1.3862944 * jax.random.uniform(splits[5], (H * HD,), jnp.float32) ** level_of(splits[5], (H * HD,), ((0, 8),), -0.2, 0.2)), 0.5, 2.0)
    w_out = noise(splits[6], (H * HD, D), (H * HD) ** -0.5, 0.0625, ((0, 8),))
    return dict(query=query, key_in=key_in, value=value, gate=gate, kv_start=kv_start, norm_gain=norm_gain, w_out=w_out)


def reference(query, key_in, value, gate, kv_start, norm_gain, w_out):
    block = min(512, TOK_DEV)
    count = TOKENS // block
    highest = lax.Precision.HIGHEST

    def step(state, index):
        start = (index * block).astype(jnp.int32)
        q_blk = lax.dynamic_slice_in_dim(query, start, block, 0).astype(jnp.float32)
        k_blk = lax.dynamic_slice_in_dim(key_in, start, block, 0).astype(jnp.float32)
        v_blk = lax.dynamic_slice_in_dim(value, start, block, 0)
        qa = jax.nn.silu(q_blk).astype(jnp.bfloat16).reshape(block, H, HD).astype(jnp.float32)
        ka = jax.nn.silu(k_blk).astype(jnp.bfloat16).reshape(block, H, HD).astype(jnp.float32)
        va = v_blk.reshape(block, H, HD).astype(jnp.float32)
        inter = jnp.einsum('thd,hde->the', qa, state, precision=highest)
        scores = jnp.einsum('thd,shd->hts', qa, ka, precision=highest)
        causal = jnp.arange(block)[:, None] >= jnp.arange(block)[None, :]
        scores = jnp.where(causal[None], scores, jnp.float32(0.0))
        intra = jnp.einsum('hts,she->the', scores, va, precision=highest)
        new_state = state + jnp.einsum('thd,the->hde', ka, va, precision=highest)
        return (new_state, inter + intra)
    _, outputs = lax.scan(step, kv_start.astype(jnp.float32), jnp.arange(count))
    heads_out = outputs.reshape(TOKENS, H, HD)
    scale = lax.rsqrt(lax.optimization_barrier(jnp.mean(heads_out * heads_out, axis=-1, keepdims=True)) + 1e-05)
    normed = (heads_out * scale).reshape(TOKENS, H * HD)
    attn = (normed * norm_gain[None, :] * jax.nn.sigmoid(gate.astype(jnp.float32))).astype(jnp.bfloat16)
    width = H * HD // N_TP
    total = jnp.zeros((TOKENS, D), jnp.float32)
    for group in range(N_TP):
        part = jnp.dot(attn[:, group * width:(group + 1) * width], w_out[group * width:(group + 1) * width], preferred_element_type=jnp.float32)
        total = total + part.astype(jnp.bfloat16).astype(jnp.float32)
    return total.astype(jnp.bfloat16)
```

```python
import functools

import jax
import jax.numpy as jnp
from jax import lax
from jax.experimental import pallas as pl
from jax.experimental.pallas import tpu as pltpu
from jax.sharding import PartitionSpec as P

HD = 128
MESH = pl.DeviceIdType.MESH


def other_chip(at):
    return {"tp": at}


def project_kernel(
    chips, a_ref, w_hbm, o_ref, w_ref, pair_out, pair_in, line_out, from_low, from_high, acc,
    w_sem, pair_out_sem, pair_in_sem, up_sem, low_sem, down_sem, high_sem,
):
    pieces, _, width = w_ref.shape
    rows = o_ref.shape[0]
    me = lax.axis_index("tp")
    z, core = me // 2, me % 2
    sibling = me + 1 - 2 * core
    top = chips - 1

    def weights(k):
        return pltpu.make_async_copy(
            w_hbm.at[:, pl.ds(pl.multiple_of(k * width, width), width)], w_ref.at[k], w_sem.at[k]
        )

    for k in range(pieces):
        weights(k).start()

    barrier = pltpu.get_barrier_semaphore()
    pl.semaphore_signal(barrier, inc=1, device_id=other_chip(sibling), device_id_type=MESH)

    @pl.when(z > 0)
    def _():
        pl.semaphore_signal(barrier, inc=1, device_id=other_chip(me - 2), device_id_type=MESH)

    @pl.when(z < top)
    def _():
        pl.semaphore_signal(barrier, inc=1, device_id=other_chip(me + 2), device_id_type=MESH)

    pl.semaphore_wait(barrier, 1 + jnp.minimum(z, 1) + jnp.minimum(top - z, 1))

    def partial(d, side, k):
        at = pl.multiple_of((2 * d + side) * rows, rows)
        return jnp.dot(a_ref[pl.ds(at, rows), :], w_ref[k], preferred_element_type=jnp.float32)

    def pair_copy(i):
        return pltpu.make_async_remote_copy(
            src_ref=pair_out.at[i], dst_ref=pair_in.at[i],
            send_sem=pair_out_sem.at[i], recv_sem=pair_in_sem.at[i],
            device_id=other_chip(sibling), device_id_type=MESH,
        )

    def up_copy(s):
        return pltpu.make_async_remote_copy(
            src_ref=line_out.at[(top - s // pieces) * pieces + s % pieces], dst_ref=from_low.at[s],
            send_sem=up_sem.at[s], recv_sem=low_sem.at[s],
            device_id=other_chip(me + 2), device_id_type=MESH,
        )

    def down_copy(s):
        return pltpu.make_async_remote_copy(
            src_ref=line_out.at[s], dst_ref=from_high.at[s],
            send_sem=down_sem.at[s], recv_sem=high_sem.at[s],
            device_id=other_chip(me - 2), device_id_type=MESH,
        )

    def chip_sum(d, k):
        i = d * pieces + k
        pair_out[i] = partial(d, 1 - core, k).astype(pair_out.dtype)
        copy = pair_copy(i)
        copy.start()
        mine = partial(d, core, k)
        copy.wait_recv()
        return mine + pair_in[i].astype(jnp.float32)

    def slot(s, carry):
        k = s % pieces
        turn = s // pieces

        @pl.when(s < pieces)
        def _():
            weights(k).wait()

        @pl.when(top - turn > z)
        def _():
            d = top - turn
            i = d * pieces + k
            total = chip_sum(d, k)

            @pl.when(z > 0)
            def _():
                up_copy(s).wait_recv()
                line_out[i] = (total + from_low[s].astype(jnp.float32)).astype(line_out.dtype)

            @pl.when(z == 0)
            def _():
                line_out[i] = total.astype(line_out.dtype)

            @pl.when(s >= 2)
            def _():
                up_copy(s - 2).wait_send()

            up_copy(s).start()

        @pl.when(turn < z)
        def _():
            total = chip_sum(turn, k)

            @pl.when(z < top)
            def _():
                down_copy(s).wait_recv()
                line_out[s] = (total + from_high[s].astype(jnp.float32)).astype(line_out.dtype)

            @pl.when(z == top)
            def _():
                line_out[s] = total.astype(line_out.dtype)

            @pl.when(s >= 2)
            def _():
                down_copy(s - 2).wait_send()

            down_copy(s).start()

        @pl.when(turn == 1)
        def _():
            acc[k] = chip_sum(z, k)

        return carry

    lax.fori_loop(0, top * pieces, slot, 0)

    def finish(k, carry):
        up_at = (top - z) * pieces + k
        down_at = z * pieces + k

        @pl.when(z < top)
        def _():
            down_copy(down_at).wait_recv()
            acc[k] = acc[k] + from_high[down_at].astype(jnp.float32)

        @pl.when(z > 0)
        def _():
            up_copy(up_at).wait_recv()
            acc[k] = acc[k] + from_low[up_at].astype(jnp.float32)

        o_ref[:, pl.ds(pl.multiple_of(k * width, width), width)] = acc[k].astype(o_ref.dtype)
        return carry

    lax.fori_loop(0, pieces, finish, 0)

    for back in (2, 1):
        @pl.when(z < top)
        def _():
            up_copy((top - z) * pieces - back).wait_send()

        @pl.when(z > 0)
        def _():
            down_copy(z * pieces - back).wait_send()

    def drain(i, carry):
        pair_copy(i).wait_send()
        return carry

    lax.fori_loop(0, chips * pieces, drain, 0)


def project(attn, w_out, n_tp):
    depth, columns = w_out.shape
    rows = attn.shape[0] // n_tp
    chips = n_tp // 2
    width = 1024
    pieces = columns // width
    every, passing = chips * pieces, (chips - 1) * pieces
    chunk = lambda n: pltpu.VMEM((n, rows, width), jnp.bfloat16)
    dma = lambda n: pltpu.SemaphoreType.DMA((n,))
    return pl.pallas_call(
        functools.partial(project_kernel, chips),
        out_shape=jax.ShapeDtypeStruct((rows, columns), jnp.bfloat16),
        in_specs=[pl.BlockSpec(memory_space=pltpu.VMEM), pl.BlockSpec(memory_space=pl.ANY)],
        out_specs=pl.BlockSpec(memory_space=pltpu.VMEM),
        scratch_shapes=[
            pltpu.VMEM((pieces, depth, width), jnp.bfloat16),
            chunk(every), chunk(every), chunk(every), chunk(passing), chunk(passing),
            pltpu.VMEM((pieces, rows, width), jnp.float32),
            dma(pieces), dma(every), dma(every),
            dma(passing), dma(passing), dma(passing), dma(passing),
        ],
        compiler_params=pltpu.CompilerParams(
            collective_id=0, has_side_effects=True, vmem_limit_bytes=60 * 2**20
        ),
        cost_estimate=pl.CostEstimate(
            flops=2 * attn.shape[0] * depth * columns, bytes_accessed=2 * depth * columns,
            transcendentals=0,
        ),
    )(attn, w_out)


def per_device(n_tp, query, key_in, value, gate, kv_start, norm_gain, w_out):
    rows = query.shape[0]
    heads = query.shape[1] // HD
    block = min(512, rows)
    count = rows // block
    highest = lax.Precision.HIGHEST
    qa = (
        jax.nn.silu(query.astype(jnp.float32)).astype(jnp.bfloat16).reshape(count, block, heads, HD)
    )
    ka = (
        jax.nn.silu(key_in.astype(jnp.float32))
        .astype(jnp.bfloat16)
        .reshape(count, block, heads, HD)
    )
    va = value.reshape(count, block, heads, HD)
    block_states = jnp.einsum("nthd,nthe->nhde", ka, va, preferred_element_type=jnp.float32)
    own_total = jnp.sum(block_states, axis=0)
    local_before = jnp.cumsum(block_states, axis=0) - block_states
    gathered = lax.all_gather(
        own_total[None].astype(jnp.bfloat16), "seq", axis=0, tiled=True
    ).astype(jnp.float32)
    position = lax.axis_index("seq")
    below = (jnp.arange(gathered.shape[0]) < position).astype(jnp.float32)
    prior = jnp.sum(gathered * below[:, None, None, None], axis=0)
    states = local_before + (kv_start + prior)[None]
    q_float = qa.astype(jnp.float32)
    inter = jnp.einsum("nthd,nhde->nthe", q_float, states, precision=highest)
    scores = jnp.einsum("nthd,nshd->nhts", qa, ka, preferred_element_type=jnp.float32)
    causal = jnp.arange(block)[:, None] >= jnp.arange(block)[None, :]
    scores = jnp.where(causal[None, None], scores, jnp.float32(0.0))
    intra = jnp.einsum("nhts,nshe->nthe", scores, va.astype(jnp.float32), precision=highest)
    heads_out = (inter + intra).reshape(rows, heads, HD)
    scale = lax.rsqrt(jnp.mean(heads_out * heads_out, axis=-1, keepdims=True) + 1e-05)
    normed = (heads_out * scale).reshape(rows, heads * HD)
    attn = (normed * norm_gain[None, :] * jax.nn.sigmoid(gate.astype(jnp.float32))).astype(
        jnp.bfloat16
    )
    return project(attn, w_out, n_tp)


def solution(mesh):
    in_specs = (
        P("seq", "tp"),
        P("seq", "tp"),
        P("seq", "tp"),
        P("seq", "tp"),
        P("tp", None, None),
        P("tp"),
        P("tp", None),
    )
    out_specs = P(("seq", "tp"), None)
    return jax.shard_map(
        functools.partial(per_device, mesh.shape["tp"]), mesh=mesh, in_specs=in_specs, out_specs=out_specs, check_vma=False
    )
```

```python
import functools

import jax
import jax.numpy as jnp
from jax import lax
from jax.experimental import pallas as pl
from jax.experimental.pallas import tpu as pltpu
from jax.sharding import PartitionSpec as P

HD = 128
MESH = pl.DeviceIdType.MESH


def project_kernel(
    chips, a_ref, w_hbm, o_ref, w_ref, pair_out, pair_in, own, from_low, from_high, acc,
    w_sem, pair_out_sem, pair_in_sem, up_sem, low_sem, down_sem, high_sem,
):
    pieces, depth, width = w_ref.shape
    rows = o_ref.shape[0]
    me = lax.axis_index("tp")
    z, core = me // 2, me % 2
    sibling = me + 1 - 2 * core
    top = chips - 1

    def weights(k):
        return pltpu.make_async_copy(
            w_hbm.at[:, pl.ds(pl.multiple_of(k * width, width), width)], w_ref.at[k], w_sem.at[k]
        )

    for k in range(pieces):
        weights(k).start()

    barrier = pltpu.get_barrier_semaphore()
    pl.semaphore_signal(barrier, inc=1, device_id={"tp": sibling}, device_id_type=MESH)

    @pl.when(z > 0)
    def _():
        pl.semaphore_signal(barrier, inc=1, device_id={"tp": me - 2}, device_id_type=MESH)

    @pl.when(z < top)
    def _():
        pl.semaphore_signal(barrier, inc=1, device_id={"tp": me + 2}, device_id_type=MESH)

    pl.semaphore_wait(barrier, 1 + jnp.minimum(z, 1) + jnp.minimum(top - z, 1))

    def pair_copy(k):
        return pltpu.make_async_remote_copy(
            src_ref=pair_out.at[k], dst_ref=pair_in.at[k],
            send_sem=pair_out_sem.at[k], recv_sem=pair_in_sem.at[k],
            device_id={"tp": sibling}, device_id_type=MESH,
        )

    def up_copy(k, j):
        return pltpu.make_async_remote_copy(
            src_ref=own.at[k, top - j], dst_ref=from_low.at[k, j],
            send_sem=up_sem.at[k, j], recv_sem=low_sem.at[k, j],
            device_id={"tp": me + 2}, device_id_type=MESH,
        )

    def down_copy(k, j):
        return pltpu.make_async_remote_copy(
            src_ref=own.at[k, j], dst_ref=from_high.at[k, j],
            send_sem=down_sem.at[k, j], recv_sem=high_sem.at[k, j],
            device_id={"tp": me - 2}, device_id_type=MESH,
        )

    def partial(k, side):
        a = a_ref[:, side].reshape(chips * rows, depth)
        out = jnp.dot(a, w_ref[k], preferred_element_type=jnp.float32)
        return out.astype(own.dtype).reshape(chips, rows, width)

    def compute(k):
        weights(k).wait()
        pair_out[k] = partial(k, 1 - core)
        pair_copy(k).start()
        own[k] = partial(k, core)

    def chip_sum(k, d):
        return own[k, d].astype(jnp.float32) + pair_in[k, d].astype(jnp.float32)

    def pass_on(k):
        pair_copy(k).wait_recv()
        for j in range(top):
            up, down = top - j, j

            @pl.when(up > z)
            def _():
                @pl.when(z > 0)
                def _():
                    up_copy(k, j).wait_recv()
                    total = chip_sum(k, up) + from_low[k, j].astype(jnp.float32)
                    own[k, up] = total.astype(own.dtype)

                @pl.when(z == 0)
                def _():
                    own[k, up] = chip_sum(k, up).astype(own.dtype)

                @pl.when(k >= 1)
                def _():
                    up_copy(k - 1, j).wait_send()

                up_copy(k, j).start()

            @pl.when(down < z)
            def _():
                @pl.when(z < top)
                def _():
                    down_copy(k, j).wait_recv()
                    total = chip_sum(k, down) + from_high[k, j].astype(jnp.float32)
                    own[k, down] = total.astype(own.dtype)

                @pl.when(z == top)
                def _():
                    own[k, down] = chip_sum(k, down).astype(own.dtype)

                @pl.when(k >= 1)
                def _():
                    down_copy(k - 1, j).wait_send()

                down_copy(k, j).start()

    def finish(k):
        acc[...] = chip_sum(k, z)

        @pl.when(z < top)
        def _():
            down_copy(k, z).wait_recv()
            acc[...] = acc[...] + from_high[k, z].astype(jnp.float32)

        @pl.when(z > 0)
        def _():
            up_copy(k, top - z).wait_recv()
            acc[...] = acc[...] + from_low[k, top - z].astype(jnp.float32)

        o_ref[:, pl.ds(pl.multiple_of(k * width, width), width)] = acc[...].astype(o_ref.dtype)

    def step(k, carry):
        @pl.when(k < pieces)
        def _():
            compute(k)

        @pl.when((k >= 1) & (k <= pieces))
        def _():
            pass_on(k - 1)

        @pl.when(k >= 2)
        def _():
            finish(k - 2)

        return carry

    lax.fori_loop(0, pieces + 2, step, 0)

    for j in range(top):
        @pl.when(top - j > z)
        def _():
            up_copy(pieces - 1, j).wait_send()

        @pl.when(j < z)
        def _():
            down_copy(pieces - 1, j).wait_send()

    def drain(k, carry):
        pair_copy(k).wait_send()
        return carry

    lax.fori_loop(0, pieces, drain, 0)


def project(attn, w_out, n_tp):
    depth, columns = w_out.shape
    rows = attn.shape[0] // n_tp
    chips = n_tp // 2
    width = 512
    pieces = columns // width
    chunk = lambda n: pltpu.VMEM((pieces, n, rows, width), jnp.bfloat16)
    dma = lambda *n: pltpu.SemaphoreType.DMA(n)
    return pl.pallas_call(
        functools.partial(project_kernel, chips),
        out_shape=jax.ShapeDtypeStruct((rows, columns), jnp.bfloat16),
        in_specs=[pl.BlockSpec(memory_space=pltpu.VMEM), pl.BlockSpec(memory_space=pl.ANY)],
        out_specs=pl.BlockSpec(memory_space=pltpu.VMEM),
        scratch_shapes=[
            pltpu.VMEM((pieces, depth, width), jnp.bfloat16),
            chunk(chips), chunk(chips), chunk(chips), chunk(chips - 1), chunk(chips - 1),
            pltpu.VMEM((rows, width), jnp.float32),
            dma(pieces), dma(pieces), dma(pieces),
            dma(pieces, chips - 1), dma(pieces, chips - 1),
            dma(pieces, chips - 1), dma(pieces, chips - 1),
        ],
        compiler_params=pltpu.CompilerParams(
            collective_id=0, has_side_effects=True, vmem_limit_bytes=60 * 2**20
        ),
        cost_estimate=pl.CostEstimate(
            flops=2 * attn.shape[0] * depth * columns, bytes_accessed=2 * depth * columns,
            transcendentals=0,
        ),
    )(attn.reshape(chips, 2, rows, depth), w_out)


def per_device(n_tp, query, key_in, value, gate, kv_start, norm_gain, w_out):
    rows = query.shape[0]
    heads = query.shape[1] // HD
    block = min(512, rows)
    count = rows // block
    highest = lax.Precision.HIGHEST
    qa = (
        jax.nn.silu(query.astype(jnp.float32)).astype(jnp.bfloat16).reshape(count, block, heads, HD)
    )
    ka = (
        jax.nn.silu(key_in.astype(jnp.float32))
        .astype(jnp.bfloat16)
        .reshape(count, block, heads, HD)
    )
    va = value.reshape(count, block, heads, HD)
    block_states = jnp.einsum("nthd,nthe->nhde", ka, va, preferred_element_type=jnp.float32)
    own_total = jnp.sum(block_states, axis=0)
    local_before = jnp.cumsum(block_states, axis=0) - block_states
    gathered = lax.all_gather(
        own_total[None].astype(jnp.bfloat16), "seq", axis=0, tiled=True
    ).astype(jnp.float32)
    position = lax.axis_index("seq")
    below = (jnp.arange(gathered.shape[0]) < position).astype(jnp.float32)
    prior = jnp.sum(gathered * below[:, None, None, None], axis=0)
    states = local_before + (kv_start + prior)[None]
    q_float = qa.astype(jnp.float32)
    inter = jnp.einsum("nthd,nhde->nthe", q_float, states, precision=highest)
    scores = jnp.einsum("nthd,nshd->nhts", qa, ka, preferred_element_type=jnp.float32)
    causal = jnp.arange(block)[:, None] >= jnp.arange(block)[None, :]
    scores = jnp.where(causal[None, None], scores, jnp.float32(0.0))
    intra = jnp.einsum("nhts,nshe->nthe", scores, va.astype(jnp.float32), precision=highest)
    heads_out = (inter + intra).reshape(rows, heads, HD)
    scale = lax.rsqrt(jnp.mean(heads_out * heads_out, axis=-1, keepdims=True) + 1e-05)
    normed = (heads_out * scale).reshape(rows, heads * HD)
    attn = (normed * norm_gain[None, :] * jax.nn.sigmoid(gate.astype(jnp.float32))).astype(
        jnp.bfloat16
    )
    return project(attn, w_out, n_tp)


def solution(mesh):
    in_specs = (
        P("seq", "tp"),
        P("seq", "tp"),
        P("seq", "tp"),
        P("seq", "tp"),
        P("tp", None, None),
        P("tp"),
        P("tp", None),
    )
    out_specs = P(("seq", "tp"), None)
    return jax.shard_map(
        functools.partial(per_device, mesh.shape["tp"]), mesh=mesh, in_specs=in_specs, out_specs=out_specs, check_vma=False
    )
```

```python
import functools

import jax
import jax.numpy as jnp
from jax import lax
from jax.experimental import pallas as pl
from jax.experimental.pallas import tpu as pltpu
from jax.sharding import PartitionSpec as P

HD = 128
MESH = pl.DeviceIdType.MESH


def project_kernel(
    chips, a_ref, w_hbm, o_ref, w_ref, pair_out, pair_in, own, from_low, from_high,
    w_sem, pair_out_sem, pair_in_sem, up_sem, low_sem, down_sem, high_sem,
):
    pieces, depth, width = w_ref.shape
    rows = o_ref.shape[0]
    me = lax.axis_index("tp")
    z, core = me // 2, me % 2
    sibling = me + 1 - 2 * core
    above = lax.rem(z + 1, chips) * 2 + core
    below = lax.rem(z + chips - 1, chips) * 2 + core
    half = chips // 2

    def weights(k):
        return pltpu.make_async_copy(
            w_hbm.at[:, pl.ds(pl.multiple_of(k * width, width), width)], w_ref.at[k], w_sem.at[k]
        )

    for k in range(pieces):
        weights(k).start()

    barrier = pltpu.get_barrier_semaphore()
    for peer in (sibling, above, below):
        pl.semaphore_signal(barrier, inc=1, device_id={"tp": peer}, device_id_type=MESH)
    pl.semaphore_wait(barrier, 3)

    def pair_copy(k):
        return pltpu.make_async_remote_copy(
            src_ref=pair_out.at[k], dst_ref=pair_in.at[k],
            send_sem=pair_out_sem.at[k], recv_sem=pair_in_sem.at[k],
            device_id={"tp": sibling}, device_id_type=MESH,
        )

    def owner_above(t):
        return lax.rem(z + t, chips)

    def owner_below(t):
        return lax.rem(z + chips - t, chips)

    def up_copy(k, t):
        return pltpu.make_async_remote_copy(
            src_ref=own.at[k, owner_above(t)], dst_ref=from_low.at[k, t - 1],
            send_sem=up_sem.at[k, t - 1], recv_sem=low_sem.at[k, t - 1],
            device_id={"tp": above}, device_id_type=MESH,
        )

    def down_copy(k, t):
        return pltpu.make_async_remote_copy(
            src_ref=own.at[k, owner_below(t)], dst_ref=from_high.at[k, t - 1],
            send_sem=down_sem.at[k, t - 1], recv_sem=high_sem.at[k, t - 1],
            device_id={"tp": below}, device_id_type=MESH,
        )

    def partial(k, side):
        a = a_ref[:, side].reshape(chips * rows, depth)
        out = jnp.dot(a, w_ref[k], preferred_element_type=jnp.float32)
        return out.astype(own.dtype).reshape(chips, rows, width)

    def compute(k):
        weights(k).wait()
        pair_out[k] = partial(k, 1 - core)
        pair_copy(k).start()
        own[k] = partial(k, core)

    def chip_sum(k, d):
        return own[k, d].astype(jnp.float32) + pair_in[k, d].astype(jnp.float32)

    def forward(k, t, first, copy, owner, arrived):
        def begin():
            d = owner(t)
            own[k, d] = chip_sum(k, d).astype(own.dtype)
            copy(k, t).start()

        def relay():
            d = owner(t)
            copy(k, t + 1).wait_recv()
            total = chip_sum(k, d) + arrived[k, t].astype(jnp.float32)
            own[k, d] = total.astype(own.dtype)
            copy(k, t).start()

        if t == half:
            pl.when(first)(begin)
        elif t == half - 1:
            pl.when(first)(relay)
            pl.when(jnp.logical_not(first))(begin)
        else:
            relay()

    def pass_on(k):
        pair_copy(k).wait_recv()
        even = k % 2 == 0
        for t in range(half, 0, -1):
            forward(k, t, even, up_copy, owner_above, from_low)
            forward(k, t, jnp.logical_not(even), down_copy, owner_below, from_high)

    def finish(k):
        up_copy(k, 1).wait_recv()
        down_copy(k, 1).wait_recv()
        total = chip_sum(k, z) + from_low[k, 0].astype(jnp.float32)
        total = total + from_high[k, 0].astype(jnp.float32)
        o_ref[:, pl.ds(pl.multiple_of(k * width, width), width)] = total.astype(o_ref.dtype)

    def sent(k):
        for t in range(half - 1, 0, -1):
            up_copy(k, t).wait_send()
            down_copy(k, t).wait_send()

        @pl.when(k % 2 == 0)
        def _():
            up_copy(k, half).wait_send()

        @pl.when(k % 2 == 1)
        def _():
            down_copy(k, half).wait_send()

    def step(k, carry):
        @pl.when(k < pieces)
        def _():
            compute(k)

        @pl.when((k >= 3) & (k <= pieces + 2))
        def _():
            sent(k - 3)

        @pl.when((k >= 1) & (k <= pieces))
        def _():
            pass_on(k - 1)

        @pl.when((k >= 2) & (k <= pieces + 1))
        def _():
            finish(k - 2)

        return carry

    lax.fori_loop(0, pieces + 3, step, 0)

    def drain(k, carry):
        pair_copy(k).wait_send()
        return carry

    lax.fori_loop(0, pieces, drain, 0)


def project(attn, w_out, n_tp):
    depth, columns = w_out.shape
    rows = attn.shape[0] // n_tp
    chips = n_tp // 2
    width = 512
    pieces = columns // width
    chunk = lambda n: pltpu.VMEM((pieces, n, rows, width), jnp.bfloat16)
    dma = lambda *n: pltpu.SemaphoreType.DMA(n)
    return pl.pallas_call(
        functools.partial(project_kernel, chips),
        out_shape=jax.ShapeDtypeStruct((rows, columns), jnp.bfloat16),
        in_specs=[pl.BlockSpec(memory_space=pltpu.VMEM), pl.BlockSpec(memory_space=pl.ANY)],
        out_specs=pl.BlockSpec(memory_space=pltpu.VMEM),
        scratch_shapes=[
            pltpu.VMEM((pieces, depth, width), jnp.bfloat16),
            chunk(chips), chunk(chips), chunk(chips), chunk(chips // 2), chunk(chips // 2),
            dma(pieces), dma(pieces), dma(pieces),
            dma(pieces, chips // 2), dma(pieces, chips // 2),
            dma(pieces, chips // 2), dma(pieces, chips // 2),
        ],
        compiler_params=pltpu.CompilerParams(
            collective_id=0, has_side_effects=True, vmem_limit_bytes=60 * 2**20
        ),
        cost_estimate=pl.CostEstimate(
            flops=2 * attn.shape[0] * depth * columns, bytes_accessed=2 * depth * columns,
            transcendentals=0,
        ),
    )(attn.reshape(chips, 2, rows, depth), w_out)


def per_device(n_tp, query, key_in, value, gate, kv_start, norm_gain, w_out):
    rows = query.shape[0]
    heads = query.shape[1] // HD
    block = min(512, rows)
    count = rows // block
    highest = lax.Precision.HIGHEST
    qa = (
        jax.nn.silu(query.astype(jnp.float32)).astype(jnp.bfloat16).reshape(count, block, heads, HD)
    )
    ka = (
        jax.nn.silu(key_in.astype(jnp.float32))
        .astype(jnp.bfloat16)
        .reshape(count, block, heads, HD)
    )
    va = value.reshape(count, block, heads, HD)
    block_states = jnp.einsum("nthd,nthe->nhde", ka, va, preferred_element_type=jnp.float32)
    own_total = jnp.sum(block_states, axis=0)
    local_before = jnp.cumsum(block_states, axis=0) - block_states
    gathered = lax.all_gather(
        own_total[None].astype(jnp.bfloat16), "seq", axis=0, tiled=True
    ).astype(jnp.float32)
    position = lax.axis_index("seq")
    below = (jnp.arange(gathered.shape[0]) < position).astype(jnp.float32)
    prior = jnp.sum(gathered * below[:, None, None, None], axis=0)
    states = local_before + (kv_start + prior)[None]
    q_float = qa.astype(jnp.float32)
    inter = jnp.einsum("nthd,nhde->nthe", q_float, states, precision=highest)
    scores = jnp.einsum("nthd,nshd->nhts", qa, ka, preferred_element_type=jnp.float32)
    causal = jnp.arange(block)[:, None] >= jnp.arange(block)[None, :]
    scores = jnp.where(causal[None, None], scores, jnp.float32(0.0))
    intra = jnp.einsum("nhts,nshe->nthe", scores, va.astype(jnp.float32), precision=highest)
    heads_out = (inter + intra).reshape(rows, heads, HD)
    scale = lax.rsqrt(jnp.mean(heads_out * heads_out, axis=-1, keepdims=True) + 1e-05)
    normed = (heads_out * scale).reshape(rows, heads * HD)
    attn = (normed * norm_gain[None, :] * jax.nn.sigmoid(gate.astype(jnp.float32))).astype(
        jnp.bfloat16
    )
    return project(attn, w_out, n_tp)


def solution(mesh):
    in_specs = (
        P("seq", "tp"),
        P("seq", "tp"),
        P("seq", "tp"),
        P("seq", "tp"),
        P("tp", None, None),
        P("tp"),
        P("tp", None),
    )
    out_specs = P(("seq", "tp"), None)
    return jax.shard_map(
        functools.partial(per_device, mesh.shape["tp"]), mesh=mesh, in_specs=in_specs, out_specs=out_specs, check_vma=False
    )
```

```python
import functools

import jax
import jax.numpy as jnp
from jax import lax
from jax.experimental import pallas as pl
from jax.experimental.pallas import tpu as pltpu
from jax.sharding import PartitionSpec as P

HD = 128
MESH = pl.DeviceIdType.MESH


def sigmoid(u):
    return 0.5 + 0.5 * jnp.tanh(0.5 * u)


def attend_kernel(
    n_seq, block, q_ref, k_ref, v_ref, g_ref, kv_ref, gain_ref, o_ref,
    qa_ref, ka_ref, local, prefix, state, own_sum, arrived, send_sem, recv_sem,
):
    me = lax.axis_index("seq")
    heads = kv_ref.shape[0]
    count = q_ref.shape[0] // block
    blocks = [slice(n * block, (n + 1) * block) for n in range(count)]
    f32 = jnp.float32

    barrier = pltpu.get_barrier_semaphore()
    for p in range(n_seq):
        @pl.when(p != me)
        def _():
            pl.semaphore_signal(barrier, inc=1, device_id={"seq": p}, device_id_type=MESH)

    def lanes(h):
        return pl.ds(pl.multiple_of(h * HD, HD), HD)

    def sums(h, carry):
        total = jnp.zeros((HD, HD), f32)
        for n, rows in enumerate(blocks):
            u = k_ref[rows, lanes(h)].astype(f32)
            ka = (u * sigmoid(u)).astype(jnp.bfloat16)
            ka_ref[rows, lanes(h)] = ka
            prefix[h, n] = total.astype(jnp.bfloat16)
            total += lax.dot_general(
                ka, v_ref[rows, lanes(h)], (((0,), (0,)), ((), ())), preferred_element_type=f32
            )
        own_sum[h] = total.astype(jnp.bfloat16)
        return carry

    lax.fori_loop(0, heads, sums, 0)
    pl.semaphore_wait(barrier, n_seq - 1)

    def copy_to(p):
        return pltpu.make_async_remote_copy(
            src_ref=own_sum, dst_ref=arrived.at[me],
            send_sem=send_sem.at[p], recv_sem=recv_sem.at[me],
            device_id={"seq": p}, device_id_type=MESH,
        )

    def copy_from(p):
        return pltpu.make_async_remote_copy(
            src_ref=own_sum, dst_ref=arrived.at[p],
            send_sem=send_sem.at[p], recv_sem=recv_sem.at[p],
            device_id={"seq": p}, device_id_type=MESH,
        )

    for p in range(n_seq - 1, -1, -1):
        @pl.when(p > me)
        def _():
            copy_to(p).start()

    above = lax.broadcasted_iota(jnp.int32, (block, block), 0) >= lax.broadcasted_iota(
        jnp.int32, (block, block), 1
    )

    def within(h, carry):
        for n, rows in enumerate(blocks):
            u = q_ref[rows, lanes(h)].astype(f32)
            qa = (u * sigmoid(u)).astype(jnp.bfloat16)
            qa_ref[rows, lanes(h)] = qa
            scores = lax.dot_general(
                qa, ka_ref[rows, lanes(h)], (((1,), (1,)), ((), ())), preferred_element_type=f32
            )
            scores = jnp.where(above, scores, 0.0).astype(jnp.bfloat16)
            out = jnp.dot(scores, v_ref[rows, lanes(h)], preferred_element_type=f32)
            if n > 0:
                out += jnp.dot(qa, prefix[h, n], preferred_element_type=f32)
            local[rows, lanes(h)] = out
        return carry

    lax.fori_loop(0, heads, within, 0)

    state[...] = kv_ref[...]
    for p in range(n_seq):
        @pl.when(p < me)
        def _():
            copy_from(p).wait_recv()
            state[...] += arrived[p].astype(f32)

    def outputs(h, carry):
        high = state[h].astype(jnp.bfloat16)
        low = (state[h] - high.astype(f32)).astype(jnp.bfloat16)
        gain = gain_ref[:, lanes(h)]
        for rows in blocks:
            qa = qa_ref[rows, lanes(h)]
            out = local[rows, lanes(h)] + jnp.dot(qa, high, preferred_element_type=f32)
            out += jnp.dot(qa, low, preferred_element_type=f32)
            scale = lax.rsqrt(jnp.mean(out * out, axis=-1, keepdims=True) + 1e-05)
            gate = sigmoid(g_ref[rows, lanes(h)].astype(f32))
            o_ref[rows, lanes(h)] = (out * scale * gain * gate).astype(o_ref.dtype)
        return carry

    lax.fori_loop(0, heads, outputs, 0)

    for p in range(n_seq):
        @pl.when(p > me)
        def _():
            copy_to(p).wait_send()


def attend(query, key_in, value, gate, kv_start, norm_gain, n_seq):
    rows, columns = query.shape
    heads = columns // HD
    block = min(256, rows)
    vmem = pl.BlockSpec(memory_space=pltpu.VMEM)
    bf16, f32 = jnp.bfloat16, jnp.float32
    return pl.pallas_call(
        functools.partial(attend_kernel, n_seq, block),
        out_shape=jax.ShapeDtypeStruct((rows, columns), bf16),
        in_specs=[vmem] * 6,
        out_specs=vmem,
        scratch_shapes=[
            pltpu.VMEM((rows, columns), bf16),
            pltpu.VMEM((rows, columns), bf16),
            pltpu.VMEM((rows, columns), f32),
            pltpu.VMEM((heads, rows // block, HD, HD), bf16),
            pltpu.VMEM((heads, HD, HD), f32),
            pltpu.VMEM((heads, HD, HD), bf16),
            pltpu.VMEM((n_seq, heads, HD, HD), bf16),
            pltpu.SemaphoreType.DMA((n_seq,)),
            pltpu.SemaphoreType.DMA((n_seq,)),
        ],
        compiler_params=pltpu.CompilerParams(
            collective_id=1, has_side_effects=True, vmem_limit_bytes=60 * 2**20
        ),
        cost_estimate=pl.CostEstimate(
            flops=8 * rows * block * columns, bytes_accessed=10 * rows * columns,
            transcendentals=3 * rows * columns,
        ),
    )(query, key_in, value, gate, kv_start, norm_gain.reshape(1, columns))


def project_kernel(
    chips, a_ref, w_hbm, o_ref, w_ref, pair_out, pair_in, own, from_low, from_high,
    w_sem, pair_out_sem, pair_in_sem, up_sem, low_sem, down_sem, high_sem,
):
    pieces, depth, width = w_ref.shape
    rows = o_ref.shape[0]
    me = lax.axis_index("tp")
    z, core = me // 2, me % 2
    sibling = me + 1 - 2 * core
    above = lax.rem(z + 1, chips) * 2 + core
    below = lax.rem(z + chips - 1, chips) * 2 + core
    half = chips // 2

    def weights(k):
        return pltpu.make_async_copy(
            w_hbm.at[:, pl.ds(pl.multiple_of(k * width, width), width)], w_ref.at[k], w_sem.at[k]
        )

    for k in range(pieces):
        weights(k).start()

    barrier = pltpu.get_barrier_semaphore()
    for peer in (sibling, above, below):
        pl.semaphore_signal(barrier, inc=1, device_id={"tp": peer}, device_id_type=MESH)
    pl.semaphore_wait(barrier, 3)

    def pair_copy(k):
        return pltpu.make_async_remote_copy(
            src_ref=pair_out.at[k], dst_ref=pair_in.at[k],
            send_sem=pair_out_sem.at[k], recv_sem=pair_in_sem.at[k],
            device_id={"tp": sibling}, device_id_type=MESH,
        )

    def owner_above(t):
        return lax.rem(z + t, chips)

    def owner_below(t):
        return lax.rem(z + chips - t, chips)

    def up_copy(k, t):
        return pltpu.make_async_remote_copy(
            src_ref=own.at[k, owner_above(t)], dst_ref=from_low.at[k, t - 1],
            send_sem=up_sem.at[k, t - 1], recv_sem=low_sem.at[k, t - 1],
            device_id={"tp": above}, device_id_type=MESH,
        )

    def down_copy(k, t):
        return pltpu.make_async_remote_copy(
            src_ref=own.at[k, owner_below(t)], dst_ref=from_high.at[k, t - 1],
            send_sem=down_sem.at[k, t - 1], recv_sem=high_sem.at[k, t - 1],
            device_id={"tp": below}, device_id_type=MESH,
        )

    def partial(k, side):
        a = a_ref[:, side].reshape(chips * rows, depth)
        out = jnp.dot(a, w_ref[k], preferred_element_type=jnp.float32)
        return out.astype(own.dtype).reshape(chips, rows, width)

    def compute(k):
        weights(k).wait()
        pair_out[k] = partial(k, 1 - core)
        pair_copy(k).start()
        own[k] = partial(k, core)

    def chip_sum(k, d):
        return own[k, d].astype(jnp.float32) + pair_in[k, d].astype(jnp.float32)

    def begin(k, t, copy, owner):
        d = owner(t)
        own[k, d] = chip_sum(k, d).astype(own.dtype)
        copy(k, t).start()

    def relay(k, t, copy, owner, arrived):
        d = owner(t)
        copy(k, t + 1).wait_recv()
        total = chip_sum(k, d) + arrived[k, t].astype(jnp.float32)
        own[k, d] = total.astype(own.dtype)
        copy(k, t).start()

    def send_first(k):
        pair_copy(k).wait_recv()

        @pl.when(k % 2 == 0)
        def _():
            begin(k, half, up_copy, owner_above)
            begin(k, half - 1, down_copy, owner_below)

        @pl.when(k % 2 == 1)
        def _():
            begin(k, half, down_copy, owner_below)
            begin(k, half - 1, up_copy, owner_above)

    def send_on(k, t):
        if t < half - 1:
            relay(k, t, up_copy, owner_above, from_low)
            relay(k, t, down_copy, owner_below, from_high)
        else:
            @pl.when(k % 2 == 0)
            def _():
                relay(k, t, up_copy, owner_above, from_low)

            @pl.when(k % 2 == 1)
            def _():
                relay(k, t, down_copy, owner_below, from_high)

    def finish(k):
        up_copy(k, 1).wait_recv()
        down_copy(k, 1).wait_recv()
        total = chip_sum(k, z) + from_low[k, 0].astype(jnp.float32)
        total = total + from_high[k, 0].astype(jnp.float32)
        o_ref[:, pl.ds(pl.multiple_of(k * width, width), width)] = total.astype(o_ref.dtype)

    def sent(k):
        for t in range(half - 1, 0, -1):
            up_copy(k, t).wait_send()
            down_copy(k, t).wait_send()

        @pl.when(k % 2 == 0)
        def _():
            up_copy(k, half).wait_send()

        @pl.when(k % 2 == 1)
        def _():
            down_copy(k, half).wait_send()

    def step(k, carry):
        def at(lag, work):
            pl.when((k >= lag) & (k < pieces + lag))(lambda: work(k - lag))

        at(0, compute)
        at(half + 2, sent)
        at(1, send_first)
        for t in range(half - 1, 0, -1):
            at(1 + half - t, functools.partial(send_on, t=t))
        at(half + 1, finish)
        return carry

    lax.fori_loop(0, pieces + half + 2, step, 0)

    def drain(k, carry):
        pair_copy(k).wait_send()
        return carry

    lax.fori_loop(0, pieces, drain, 0)


def project(attn, w_out, n_tp):
    depth, columns = w_out.shape
    rows = attn.shape[0] // n_tp
    chips = n_tp // 2
    width = 512
    pieces = columns // width
    chunk = lambda n: pltpu.VMEM((pieces, n, rows, width), jnp.bfloat16)
    dma = lambda *n: pltpu.SemaphoreType.DMA(n)
    return pl.pallas_call(
        functools.partial(project_kernel, chips),
        out_shape=jax.ShapeDtypeStruct((rows, columns), jnp.bfloat16),
        in_specs=[pl.BlockSpec(memory_space=pltpu.VMEM), pl.BlockSpec(memory_space=pl.ANY)],
        out_specs=pl.BlockSpec(memory_space=pltpu.VMEM),
        scratch_shapes=[
            pltpu.VMEM((pieces, depth, width), jnp.bfloat16),
            chunk(chips), chunk(chips), chunk(chips), chunk(chips // 2), chunk(chips // 2),
            dma(pieces), dma(pieces), dma(pieces),
            dma(pieces, chips // 2), dma(pieces, chips // 2),
            dma(pieces, chips // 2), dma(pieces, chips // 2),
        ],
        compiler_params=pltpu.CompilerParams(
            collective_id=0, has_side_effects=True, vmem_limit_bytes=60 * 2**20
        ),
        cost_estimate=pl.CostEstimate(
            flops=2 * attn.shape[0] * depth * columns, bytes_accessed=2 * depth * columns,
            transcendentals=0,
        ),
    )(attn.reshape(chips, 2, rows, depth), w_out)


def per_device(n_seq, n_tp, query, key_in, value, gate, kv_start, norm_gain, w_out):
    attn = attend(query, key_in, value, gate, kv_start, norm_gain, n_seq)
    return project(attn, w_out, n_tp)


def solution(mesh):
    in_specs = (
        P("seq", "tp"),
        P("seq", "tp"),
        P("seq", "tp"),
        P("seq", "tp"),
        P("tp", None, None),
        P("tp"),
        P("tp", None),
    )
    out_specs = P(("seq", "tp"), None)
    return jax.shard_map(
        functools.partial(per_device, mesh.shape["seq"], mesh.shape["tp"]), mesh=mesh, in_specs=in_specs, out_specs=out_specs, check_vma=False
    )
```

```python
import functools

import jax
import jax.numpy as jnp
from jax import lax
from jax.experimental import pallas as pl
from jax.experimental.pallas import tpu as pltpu
from jax.sharding import PartitionSpec as P

HD = 128
MESH = pl.DeviceIdType.MESH


def sigmoid(u):
    return 0.5 + 0.5 * jnp.tanh(0.5 * u)


def layer_kernel(
    n_seq, chips, block, q_hbm, k_hbm, v_hbm, g_hbm, kv_ref, gain_ref, w_hbm, o_ref,
    q_ref, k_ref, v_ref, a_ref, local, prefix, state, own_sum, arrived,
    w_ref, pair_out, pair_in, own, from_low, from_high,
    qg_sem, kv_sem, send_sem, recv_sem,
    w_sem, pair_out_sem, pair_in_sem, up_sem, low_sem, down_sem, high_sem,
):
    f32, bf16 = jnp.float32, jnp.bfloat16
    heads = kv_ref.shape[0]
    part = heads // 2
    blocks = [slice(n * block, (n + 1) * block) for n in range(q_ref.shape[0] // block)]
    pieces, depth, width = w_ref.shape
    rows = o_ref.shape[0]
    at_seq = lax.axis_index("seq")
    me = lax.axis_index("tp")
    z, core = me // 2, me % 2
    sibling = me + 1 - 2 * core
    above = lax.rem(z + 1, chips) * 2 + core
    below = lax.rem(z + chips - 1, chips) * 2 + core
    half = chips // 2

    def lanes(h):
        return pl.ds(pl.multiple_of(h * HD, HD), HD)

    def load_head(i, h):
        hbm, ref = ((k_hbm, k_ref), (v_hbm, v_ref))[i]
        return pltpu.make_async_copy(hbm.at[:, lanes(h)], ref.at[:, lanes(h)], kv_sem.at[i, h])

    def weights(k):
        return pltpu.make_async_copy(
            w_hbm.at[:, pl.ds(pl.multiple_of(k * width, width), width)], w_ref.at[k], w_sem.at[k]
        )

    load_q = pltpu.make_async_copy(q_hbm, q_ref, qg_sem.at[0])
    load_g = pltpu.make_async_copy(g_hbm, a_ref, qg_sem.at[1])
    for h in range(heads):
        load_head(0, h).start()
        load_head(1, h).start()
    load_q.start()
    load_g.start()

    barrier = pltpu.get_barrier_semaphore()
    for p in range(n_seq):
        @pl.when(p != at_seq)
        def _():
            pl.semaphore_signal(barrier, inc=1, device_id={"seq": p}, device_id_type=MESH)
    for peer in (sibling, above, below):
        pl.semaphore_signal(barrier, inc=1, device_id={"tp": peer}, device_id_type=MESH)

    def sums(h, carry):
        load_head(0, h).wait()
        load_head(1, h).wait()
        total = jnp.zeros((HD, HD), f32)
        for n, tokens in enumerate(blocks):
            u = k_ref[tokens, lanes(h)].astype(f32)
            ka = (u * sigmoid(u)).astype(bf16)
            k_ref[tokens, lanes(h)] = ka
            prefix[h, n] = total.astype(bf16)
            total += lax.dot_general(
                ka, v_ref[tokens, lanes(h)], (((0,), (0,)), ((), ())), preferred_element_type=f32
            )
        own_sum[h] = total.astype(bf16)
        return carry

    def state_copy(p, source, i):
        some = pl.ds(i * part, part)
        return pltpu.make_async_remote_copy(
            src_ref=own_sum.at[some], dst_ref=arrived.at[source, some],
            send_sem=send_sem.at[p, i], recv_sem=recv_sem.at[source, i],
            device_id={"seq": p}, device_id_type=MESH,
        )

    for i in range(2):
        lax.fori_loop(i * part, (i + 1) * part, sums, 0)
        if i == 0:
            pl.semaphore_wait(barrier, n_seq + 2)
        for p in range(n_seq - 1, -1, -1):
            @pl.when(p > at_seq)
            def _():
                state_copy(p, at_seq, i).start()

    for k in range(pieces):
        weights(k).start()
    load_q.wait()
    load_g.wait()

    causal = lax.broadcasted_iota(jnp.int32, (block, block), 0) >= lax.broadcasted_iota(
        jnp.int32, (block, block), 1
    )

    def within(h, carry):
        for n, tokens in enumerate(blocks):
            u = q_ref[tokens, lanes(h)].astype(f32)
            qa = (u * sigmoid(u)).astype(bf16)
            q_ref[tokens, lanes(h)] = qa
            scores = lax.dot_general(
                qa, k_ref[tokens, lanes(h)], (((1,), (1,)), ((), ())), preferred_element_type=f32
            )
            scores = jnp.where(causal, scores, 0.0).astype(bf16)
            out = jnp.dot(scores, v_ref[tokens, lanes(h)], preferred_element_type=f32)
            if n > 0:
                out += jnp.dot(qa, prefix[h, n], preferred_element_type=f32)
            local[tokens, lanes(h)] = out
        return carry

    lax.fori_loop(0, heads, within, 0)

    def outputs(h, carry):
        high = state[h].astype(bf16)
        low = (state[h] - high.astype(f32)).astype(bf16)
        gain = gain_ref[:, lanes(h)]
        for d in range(chips):
            tokens = slice(2 * d * rows, 2 * (d + 1) * rows)
            qa = q_ref[tokens, lanes(h)]
            out = local[tokens, lanes(h)] + jnp.dot(qa, high, preferred_element_type=f32)
            out += jnp.dot(qa, low, preferred_element_type=f32)
            scale = lax.rsqrt(jnp.mean(out * out, axis=-1, keepdims=True) + 1e-05)
            gate = sigmoid(a_ref[d, :, :, lanes(h)].reshape(2 * rows, HD).astype(f32))
            attn = (out * scale * gain * gate).astype(bf16)
            a_ref[d, :, :, lanes(h)] = attn.reshape(2, rows, HD)
        return carry

    state[...] = kv_ref[...]
    for i in range(2):
        some = slice(i * part, (i + 1) * part)
        for p in range(n_seq):
            @pl.when(p < at_seq)
            def _():
                state_copy(p, p, i).wait_recv()
                state[some] += arrived[p, some].astype(f32)
        lax.fori_loop(i * part, (i + 1) * part, outputs, 0)

    def pair_copy(k):
        return pltpu.make_async_remote_copy(
            src_ref=pair_out.at[k], dst_ref=pair_in.at[k],
            send_sem=pair_out_sem.at[k], recv_sem=pair_in_sem.at[k],
            device_id={"tp": sibling}, device_id_type=MESH,
        )

    def owner_above(t):
        return lax.rem(z + t, chips)

    def owner_below(t):
        return lax.rem(z + chips - t, chips)

    def up_copy(k, t):
        return pltpu.make_async_remote_copy(
            src_ref=own.at[k, owner_above(t)], dst_ref=from_low.at[k, t - 1],
            send_sem=up_sem.at[k, t - 1], recv_sem=low_sem.at[k, t - 1],
            device_id={"tp": above}, device_id_type=MESH,
        )

    def down_copy(k, t):
        return pltpu.make_async_remote_copy(
            src_ref=own.at[k, owner_below(t)], dst_ref=from_high.at[k, t - 1],
            send_sem=down_sem.at[k, t - 1], recv_sem=high_sem.at[k, t - 1],
            device_id={"tp": below}, device_id_type=MESH,
        )

    def partial(k, side):
        a = a_ref[:, side].reshape(chips * rows, depth)
        out = jnp.dot(a, w_ref[k], preferred_element_type=jnp.float32)
        return out.astype(own.dtype).reshape(chips, rows, width)

    def compute(k):
        weights(k).wait()
        pair_out[k] = partial(k, 1 - core)
        pair_copy(k).start()
        own[k] = partial(k, core)

    def chip_sum(k, d):
        return own[k, d].astype(jnp.float32) + pair_in[k, d].astype(jnp.float32)

    def begin(k, t, copy, owner):
        d = owner(t)
        own[k, d] = chip_sum(k, d).astype(own.dtype)
        copy(k, t).start()

    def relay(k, t, copy, owner, arrived):
        d = owner(t)
        copy(k, t + 1).wait_recv()
        total = chip_sum(k, d) + arrived[k, t].astype(jnp.float32)
        own[k, d] = total.astype(own.dtype)
        copy(k, t).start()

    def send_first(k):
        pair_copy(k).wait_recv()

        @pl.when(k % 2 == 0)
        def _():
            begin(k, half, up_copy, owner_above)
            begin(k, half - 1, down_copy, owner_below)

        @pl.when(k % 2 == 1)
        def _():
            begin(k, half, down_copy, owner_below)
            begin(k, half - 1, up_copy, owner_above)

    def send_on(k, t):
        if t < half - 1:
            relay(k, t, up_copy, owner_above, from_low)
            relay(k, t, down_copy, owner_below, from_high)
        else:
            @pl.when(k % 2 == 0)
            def _():
                relay(k, t, up_copy, owner_above, from_low)

            @pl.when(k % 2 == 1)
            def _():
                relay(k, t, down_copy, owner_below, from_high)

    def finish(k):
        up_copy(k, 1).wait_recv()
        down_copy(k, 1).wait_recv()
        total = chip_sum(k, z) + from_low[k, 0].astype(jnp.float32)
        total = total + from_high[k, 0].astype(jnp.float32)
        o_ref[:, pl.ds(pl.multiple_of(k * width, width), width)] = total.astype(o_ref.dtype)

    def sent(k):
        for t in range(half - 1, 0, -1):
            up_copy(k, t).wait_send()
            down_copy(k, t).wait_send()

        @pl.when(k % 2 == 0)
        def _():
            up_copy(k, half).wait_send()

        @pl.when(k % 2 == 1)
        def _():
            down_copy(k, half).wait_send()

    def step(k, carry):
        def at(lag, work):
            pl.when((k >= lag) & (k < pieces + lag))(lambda: work(k - lag))

        at(0, compute)
        at(half + 2, sent)
        at(1, send_first)
        for t in range(half - 1, 0, -1):
            at(1 + half - t, functools.partial(send_on, t=t))
        at(half + 1, finish)
        return carry

    lax.fori_loop(0, pieces + half + 2, step, 0)

    def drain(k, carry):
        pair_copy(k).wait_send()
        return carry

    lax.fori_loop(0, pieces, drain, 0)

    for p in range(n_seq):
        @pl.when(p > at_seq)
        def _():
            for i in range(2):
                state_copy(p, at_seq, i).wait_send()


def per_device(n_seq, n_tp, query, key_in, value, gate, kv_start, norm_gain, w_out):
    tokens, depth = query.shape
    columns = w_out.shape[1]
    heads = depth // HD
    rows = tokens // n_tp
    chips = n_tp // 2
    block = min(256, tokens)
    width = 256
    pieces = columns // width
    bf16, f32 = jnp.bfloat16, jnp.float32
    vmem = pl.BlockSpec(memory_space=pltpu.VMEM)
    hbm = pl.BlockSpec(memory_space=pl.ANY)
    chunk = lambda n: pltpu.VMEM((pieces, n, rows, width), bf16)
    dma = lambda *n: pltpu.SemaphoreType.DMA(n)
    return pl.pallas_call(
        functools.partial(layer_kernel, n_seq, chips, block),
        out_shape=jax.ShapeDtypeStruct((rows, columns), bf16),
        in_specs=[hbm, hbm, hbm, hbm, vmem, vmem, hbm],
        out_specs=vmem,
        scratch_shapes=[
            pltpu.VMEM((tokens, depth), bf16),
            pltpu.VMEM((tokens, depth), bf16),
            pltpu.VMEM((tokens, depth), bf16),
            pltpu.VMEM((chips, 2, rows, depth), bf16),
            pltpu.VMEM((tokens, depth), f32),
            pltpu.VMEM((heads, tokens // block, HD, HD), bf16),
            pltpu.VMEM((heads, HD, HD), f32),
            pltpu.VMEM((heads, HD, HD), bf16),
            pltpu.VMEM((n_seq, heads, HD, HD), bf16),
            pltpu.VMEM((pieces, depth, width), bf16),
            chunk(chips), chunk(chips), chunk(chips), chunk(chips // 2), chunk(chips // 2),
            dma(2), dma(2, heads), dma(n_seq, 2), dma(n_seq, 2),
            dma(pieces), dma(pieces), dma(pieces),
            dma(pieces, chips // 2), dma(pieces, chips // 2),
            dma(pieces, chips // 2), dma(pieces, chips // 2),
        ],
        compiler_params=pltpu.CompilerParams(
            collective_id=0, has_side_effects=True, vmem_limit_bytes=62 * 2**20
        ),
        cost_estimate=pl.CostEstimate(
            flops=2 * tokens * depth * (columns + 4 * block),
            bytes_accessed=2 * depth * (columns + 4 * tokens),
            transcendentals=3 * tokens * depth,
        ),
    )(
        query, key_in, value, gate.reshape(chips, 2, rows, depth), kv_start,
        norm_gain.reshape(1, depth), w_out,
    )


def solution(mesh):
    in_specs = (
        P("seq", "tp"),
        P("seq", "tp"),
        P("seq", "tp"),
        P("seq", "tp"),
        P("tp", None, None),
        P("tp"),
        P("tp", None),
    )
    out_specs = P(("seq", "tp"), None)
    return jax.shard_map(
        functools.partial(per_device, mesh.shape["seq"], mesh.shape["tp"]), mesh=mesh, in_specs=in_specs, out_specs=out_specs, check_vma=False
    )
```

```python
import functools

import jax
import jax.numpy as jnp
from jax import lax
from jax.experimental import pallas as pl
from jax.experimental.pallas import tpu as pltpu
from jax.sharding import PartitionSpec as P

HD = 128
MESH = pl.DeviceIdType.MESH


def sigmoid(u):
    return 0.5 + 0.5 * jnp.tanh(0.5 * u)


def layer_kernel(
    n_seq, chips, block, q_hbm, k_hbm, v_hbm, g_hbm, kv_ref, gain_ref, w_hbm, o_ref,
    q_ref, k_ref, v_ref, a_ref, local, prefix, state, own_sum, arrived,
    w_ref, pair_out, pair_in, own, from_low, from_high,
    qg_sem, kv_sem, send_sem, recv_sem,
    w_sem, pair_out_sem, pair_in_sem, up_sem, low_sem, down_sem, high_sem,
):
    f32, bf16 = jnp.float32, jnp.bfloat16
    heads = kv_ref.shape[0]
    part = heads // 2
    blocks = [slice(n * block, (n + 1) * block) for n in range(q_ref.shape[0] // block)]
    pieces, depth, width = w_ref.shape
    rows = o_ref.shape[0]
    at_seq = lax.axis_index("seq")
    me = lax.axis_index("tp")
    z, core = me // 2, me % 2
    sibling = me + 1 - 2 * core
    top = chips - 1
    ahead = 3

    def lanes(h):
        return pl.ds(pl.multiple_of(h * HD, HD), HD)

    def load_head(i, h):
        hbm, ref = ((k_hbm, k_ref), (v_hbm, v_ref))[i]
        return pltpu.make_async_copy(hbm.at[:, lanes(h)], ref.at[:, lanes(h)], kv_sem.at[i, h])

    def weights(k):
        return pltpu.make_async_copy(
            w_hbm.at[:, pl.ds(pl.multiple_of(k * width, width), width)], w_ref.at[k], w_sem.at[k]
        )

    load_q = pltpu.make_async_copy(q_hbm, q_ref, qg_sem.at[0])
    load_g = pltpu.make_async_copy(g_hbm, a_ref, qg_sem.at[1])
    for h in range(heads):
        load_head(0, h).start()
        load_head(1, h).start()
    load_q.start()
    load_g.start()

    barrier = pltpu.get_barrier_semaphore()
    for p in range(n_seq):
        @pl.when(p != at_seq)
        def _():
            pl.semaphore_signal(barrier, inc=1, device_id={"seq": p}, device_id_type=MESH)
    pl.semaphore_signal(barrier, inc=1, device_id={"tp": sibling}, device_id_type=MESH)

    @pl.when(z > 0)
    def _():
        pl.semaphore_signal(barrier, inc=1, device_id={"tp": me - 2}, device_id_type=MESH)

    @pl.when(z < top)
    def _():
        pl.semaphore_signal(barrier, inc=1, device_id={"tp": me + 2}, device_id_type=MESH)


    def sums(h, carry):
        load_head(0, h).wait()
        load_head(1, h).wait()
        total = jnp.zeros((HD, HD), f32)
        for n, tokens in enumerate(blocks):
            u = k_ref[tokens, lanes(h)].astype(f32)
            ka = (u * sigmoid(u)).astype(bf16)
            k_ref[tokens, lanes(h)] = ka
            prefix[h, n] = total.astype(bf16)
            total += lax.dot_general(
                ka, v_ref[tokens, lanes(h)], (((0,), (0,)), ((), ())), preferred_element_type=f32
            )
        own_sum[h] = total.astype(bf16)
        return carry

    def state_copy(p, source, i):
        some = pl.ds(i * part, part)
        return pltpu.make_async_remote_copy(
            src_ref=own_sum.at[some], dst_ref=arrived.at[source, some],
            send_sem=send_sem.at[p, i], recv_sem=recv_sem.at[source, i],
            device_id={"seq": p}, device_id_type=MESH,
        )

    for i in range(2):
        lax.fori_loop(i * part, (i + 1) * part, sums, 0)
        if i == 0:
            pl.semaphore_wait(barrier, n_seq + jnp.minimum(z, 1) + jnp.minimum(top - z, 1))
        for p in range(n_seq - 1, -1, -1):
            @pl.when(p > at_seq)
            def _():
                state_copy(p, at_seq, i).start()

    for k in range(pieces):
        weights(k).start()
    load_q.wait()
    load_g.wait()

    causal = lax.broadcasted_iota(jnp.int32, (block, block), 0) >= lax.broadcasted_iota(
        jnp.int32, (block, block), 1
    )

    def within(h, carry):
        for n, tokens in enumerate(blocks):
            u = q_ref[tokens, lanes(h)].astype(f32)
            qa = (u * sigmoid(u)).astype(bf16)
            q_ref[tokens, lanes(h)] = qa
            scores = lax.dot_general(
                qa, k_ref[tokens, lanes(h)], (((1,), (1,)), ((), ())), preferred_element_type=f32
            )
            scores = jnp.where(causal, scores, 0.0).astype(bf16)
            out = jnp.dot(scores, v_ref[tokens, lanes(h)], preferred_element_type=f32)
            if n > 0:
                out += jnp.dot(qa, prefix[h, n], preferred_element_type=f32)
            local[tokens, lanes(h)] = out
        return carry

    lax.fori_loop(0, heads, within, 0)

    def outputs(h, carry):
        high = state[h].astype(bf16)
        low = (state[h] - high.astype(f32)).astype(bf16)
        gain = gain_ref[:, lanes(h)]
        for d in range(chips):
            tokens = slice(2 * d * rows, 2 * (d + 1) * rows)
            qa = q_ref[tokens, lanes(h)]
            out = local[tokens, lanes(h)] + jnp.dot(qa, high, preferred_element_type=f32)
            out += jnp.dot(qa, low, preferred_element_type=f32)
            scale = lax.rsqrt(jnp.mean(out * out, axis=-1, keepdims=True) + 1e-05)
            gate = sigmoid(a_ref[d, :, :, lanes(h)].reshape(2 * rows, HD).astype(f32))
            attn = (out * scale * gain * gate).astype(bf16)
            a_ref[d, :, :, lanes(h)] = attn.reshape(2, rows, HD)
        return carry

    state[...] = kv_ref[...]
    for i in range(2):
        some = slice(i * part, (i + 1) * part)
        for p in range(n_seq):
            @pl.when(p < at_seq)
            def _():
                state_copy(p, p, i).wait_recv()
                state[some] += arrived[p, some].astype(f32)
        lax.fori_loop(i * part, (i + 1) * part, outputs, 0)

    def pair_copy(k):
        return pltpu.make_async_remote_copy(
            src_ref=pair_out.at[k], dst_ref=pair_in.at[k],
            send_sem=pair_out_sem.at[k], recv_sem=pair_in_sem.at[k],
            device_id={"tp": sibling}, device_id_type=MESH,
        )

    def up_copy(k, j):
        return pltpu.make_async_remote_copy(
            src_ref=own.at[k, top - j], dst_ref=from_low.at[k, j],
            send_sem=up_sem.at[k, j], recv_sem=low_sem.at[k, j],
            device_id={"tp": me + 2}, device_id_type=MESH,
        )

    def down_copy(k, j):
        return pltpu.make_async_remote_copy(
            src_ref=own.at[k, j], dst_ref=from_high.at[k, j],
            send_sem=down_sem.at[k, j], recv_sem=high_sem.at[k, j],
            device_id={"tp": me - 2}, device_id_type=MESH,
        )

    def partial(k, side):
        a = a_ref[:, side].reshape(chips * rows, depth)
        out = jnp.dot(a, w_ref[k], preferred_element_type=jnp.float32)
        return out.astype(own.dtype).reshape(chips, rows, width)

    def compute(k):
        weights(k).wait()
        pair_out[k] = partial(k, 1 - core)
        pair_copy(k).start()
        own[k] = partial(k, core)

    def chip_sum(k, d):
        return own[k, d].astype(jnp.float32) + pair_in[k, d].astype(jnp.float32)

    def send(k, j, d, copy, arrived_there, inner):
        @pl.when(inner)
        def _():
            copy(k, j).wait_recv()
            total = chip_sum(k, d) + arrived_there[k, j].astype(f32)
            own[k, d] = total.astype(own.dtype)

        @pl.when(jnp.logical_not(inner))
        def _():
            own[k, d] = chip_sum(k, d).astype(own.dtype)

        @pl.when(k >= ahead)
        def _():
            copy(k - ahead, j).wait_send()

        copy(k, j).start()

    def send_up(k):
        for j in range(top):
            pl.when(top - j > z)(lambda: send(k, j, top - j, up_copy, from_low, z > 0))

    def send_down(k):
        for j in range(top):
            pl.when(j < z)(lambda: send(k, j, j, down_copy, from_high, z < top))

    def finish(k):
        out = pl.ds(pl.multiple_of(k * width, width), width)
        total = chip_sum(k, z)

        @pl.when(z == 0)
        def _():
            down_copy(k, z).wait_recv()
            o_ref[:, out] = (total + from_high[k, 0].astype(f32)).astype(o_ref.dtype)

        @pl.when(z == top)
        def _():
            up_copy(k, 0).wait_recv()
            o_ref[:, out] = (total + from_low[k, 0].astype(f32)).astype(o_ref.dtype)

        @pl.when((z > 0) & (z < top))
        def _():
            up_copy(k, top - z).wait_recv()
            down_copy(k, z).wait_recv()
            both = from_low[k, top - z].astype(f32) + from_high[k, z].astype(f32)
            o_ref[:, out] = (total + both).astype(o_ref.dtype)

    def step(k, carry):
        def at(lag, work):
            pl.when((k >= lag) & (k < pieces + lag))(lambda: work(k - lag))

        at(0, compute)
        at(1, lambda i: pair_copy(i).wait_recv())
        at(1 + z, send_up)
        at(1 + top - z, send_down)
        at(1 + top, finish)
        return carry

    lax.fori_loop(0, pieces + top + 1, step, 0)

    for k in range(pieces - ahead, pieces):
        for j in range(top):
            pl.when(top - j > z)(lambda: up_copy(k, j).wait_send())
            pl.when(j < z)(lambda: down_copy(k, j).wait_send())

    def drain(k, carry):
        pair_copy(k).wait_send()
        return carry

    lax.fori_loop(0, pieces, drain, 0)

    for p in range(n_seq):
        @pl.when(p > at_seq)
        def _():
            for i in range(2):
                state_copy(p, at_seq, i).wait_send()


def per_device(n_seq, n_tp, query, key_in, value, gate, kv_start, norm_gain, w_out):
    tokens, depth = query.shape
    columns = w_out.shape[1]
    heads = depth // HD
    rows = tokens // n_tp
    chips = n_tp // 2
    block = min(256, tokens)
    width = 256
    pieces = columns // width
    bf16, f32 = jnp.bfloat16, jnp.float32
    vmem = pl.BlockSpec(memory_space=pltpu.VMEM)
    hbm = pl.BlockSpec(memory_space=pl.ANY)
    chunk = lambda n: pltpu.VMEM((pieces, n, rows, width), bf16)
    dma = lambda *n: pltpu.SemaphoreType.DMA(n)
    return pl.pallas_call(
        functools.partial(layer_kernel, n_seq, chips, block),
        out_shape=jax.ShapeDtypeStruct((rows, columns), bf16),
        in_specs=[hbm, hbm, hbm, hbm, vmem, vmem, hbm],
        out_specs=vmem,
        scratch_shapes=[
            pltpu.VMEM((tokens, depth), bf16),
            pltpu.VMEM((tokens, depth), bf16),
            pltpu.VMEM((tokens, depth), bf16),
            pltpu.VMEM((chips, 2, rows, depth), bf16),
            pltpu.VMEM((tokens, depth), f32),
            pltpu.VMEM((heads, tokens // block, HD, HD), bf16),
            pltpu.VMEM((heads, HD, HD), f32),
            pltpu.VMEM((heads, HD, HD), bf16),
            pltpu.VMEM((n_seq, heads, HD, HD), bf16),
            pltpu.VMEM((pieces, depth, width), bf16),
            chunk(chips), chunk(chips), chunk(chips), chunk(chips - 1), chunk(chips - 1),
            dma(2), dma(2, heads), dma(n_seq, 2), dma(n_seq, 2),
            dma(pieces), dma(pieces), dma(pieces),
            dma(pieces, chips - 1), dma(pieces, chips - 1),
            dma(pieces, chips - 1), dma(pieces, chips - 1),
        ],
        compiler_params=pltpu.CompilerParams(
            collective_id=0, has_side_effects=True, vmem_limit_bytes=62 * 2**20
        ),
        cost_estimate=pl.CostEstimate(
            flops=2 * tokens * depth * (columns + 4 * block),
            bytes_accessed=2 * depth * (columns + 4 * tokens),
            transcendentals=3 * tokens * depth,
        ),
    )(
        query, key_in, value, gate.reshape(chips, 2, rows, depth), kv_start,
        norm_gain.reshape(1, depth), w_out,
    )


def solution(mesh):
    in_specs = (
        P("seq", "tp"),
        P("seq", "tp"),
        P("seq", "tp"),
        P("seq", "tp"),
        P("tp", None, None),
        P("tp"),
        P("tp", None),
    )
    out_specs = P(("seq", "tp"), None)
    return jax.shard_map(
        functools.partial(per_device, mesh.shape["seq"], mesh.shape["tp"]), mesh=mesh, in_specs=in_specs, out_specs=out_specs, check_vma=False
    )
```
